256 devices in a mesh: rep: 16 (over z_lo, y, core), fsdp: 16 (over x, z_hi).
Axes of the slice: x: 4, y: 4, z: 8 (z_hi: 4, z_lo: 2; z = z_hi * 2 + z_lo), core: 2. Of those that a mesh axis runs over, the one named last changes fastest.
Arguments:
- activations: bfloat16 [229376, 4096], P(('rep', 'fsdp')), may hold values from -24 to 24
- cotangent: bfloat16 [229376, 1024], P(('rep', 'fsdp')), may hold values from -0.046875 to 0.046875
- momentum: float32 [16, 4096, 1024], P('rep', 'fsdp'), may hold values from -6 to 6
- band: int32 [32], replicated, may hold values from 0 to 975, as said below
Outputs:
- new_momentum: float32 [16, 4096, 1024], P('rep', 'fsdp')
- update: bfloat16 [4096, 1024], P('fsdp')
The draws below stay inside these ranges and needn't reach their ends.
Inputs may be any that keep to these rules, and one draw needn't show every extreme that they name: `band`: the 32 entries are distinct; each is u * 64 + v with u and v below 16.
All inputs are finite; a program needn't handle non-finite values.
Results may differ from the reference program's by a relative error of at most 0.015.
Values may be sent and summed in bfloat16 or wider, within the bound.
No kernel may reach another device: no remote copies, remote signals or barrier semaphores. Data moves between devices by JAX's collectives and lax.ppermute only.
A program may use at most 128 MiB of HBM per device.

```python
import math
import jax
import jax.numpy as jnp
from jax import lax

D = 4096
KV = 1024
TOK_DEV = 896
BLOCK = 64
BAND = 32
LOWFREQ = 16
REPLICAS = 16
GROUP_TOK = 14336
TOKENS = 229376
N_REP = 16
N_FSDP = 16


def draw_band(key, part):
    key = jax.random.fold_in(key, 7)
    chosen = jax.random.permutation(key, LOWFREQ * LOWFREQ)[:BAND]
    return (chosen // LOWFREQ * BLOCK + chosen % LOWFREQ).astype(jnp.int32)


def raised(result, own_key, source, target, shards_of, factor):
    def block_of(position):
        return (jnp.arange(result.shape[position]) // (result.shape[position] // shards_of)).reshape((-1,) + (1,) * (result.ndim - 1 - position))

    first = jax.random.permutation(own_key, shards_of)[block_of(target)]
    far = (block_of(target) + shards_of // 2) % shards_of
    return jnp.where((block_of(source) == first) | (block_of(source) == far), factor * result, result)


def steps_of(own_key, extent, pieces, smallest, high):
    level = 1.0
    for axis_at, blocks in pieces:
        draws = jax.random.uniform(jax.random.fold_in(jax.random.fold_in(own_key, 6), axis_at), (blocks,), jnp.float32, smallest / len(pieces), high / len(pieces))
        level = level * jnp.repeat(jnp.exp(draws), extent[axis_at] // blocks).reshape((-1,) + (1,) * (len(extent) - 1 - axis_at))
    return level


def gaussian(key, shape, scale, bound, split=(), kind=jnp.bfloat16):
    gain = steps_of(key, shape, split, -0.22, 0.18) if split else 1.0
    array = jax.random.normal(key, shape, jnp.float32) * scale * gain
    return jnp.minimum(jnp.maximum(array, -bound), bound).astype(kind)


def gaussian_with(stream_key, extent, spread, reach, shards, heavy, held_as=jnp.bfloat16):
    array = spread * jax.random.normal(stream_key, extent, jnp.float32)
    if shards:
        array = array * steps_of(stream_key, extent, shards, -0.22, 0.18)
    return jnp.clip(raised(array, jax.random.fold_in(stream_key, 3), *heavy), -reach, reach).astype(held_as)


def setup_inputs(seed: int = 0) -> dict:
    arg_keys = jax.random.split(jax.random.key(seed), 5)
    activations = gaussian_with(arg_keys[0], (TOKENS, D), 1.0, 24.0, ((0, 256),), (0, 1, 256, 6.0))
    cotangent = gaussian(arg_keys[1], (TOKENS, KV), GROUP_TOK ** -0.5, 0.046875, ((0, 256),))
    momentum = gaussian(arg_keys[2], (REPLICAS, D, KV), 1.0, 6.0, ((0, 16), (1, 16)), jnp.float32)
    band = draw_band(jax.random.fold_in(arg_keys[4], 71), 0)
    return dict(activations=activations, cotangent=cotangent, momentum=momentum, band=band)


DECAY = 0.9

def cosine_table(width):
    freq = jnp.arange(width, dtype=jnp.float32)[:, None]
    place = jnp.arange(width, dtype=jnp.float32)[None, :]
    factor = jnp.where(freq == 0, math.sqrt(1.0 / width), math.sqrt(2.0 / width))
    return factor * jnp.cos(math.pi * (2.0 * place + 1.0) * freq / (2.0 * width))

def forward_band(matrix, table, band):
    nrows, ncols = matrix.shape
    blocks = matrix.reshape(nrows // BLOCK, BLOCK, ncols // BLOCK, BLOCK)
    coeffs = jnp.einsum('ui,aibj,vj->abuv', table, blocks, table, precision=lax.Precision.HIGHEST)
    flat = coeffs.reshape(nrows // BLOCK, ncols // BLOCK, BLOCK * BLOCK)
    return flat[:, :, band]

def inverse_band(values, table, band, nrows, ncols):
    grid = jnp.zeros((nrows // BLOCK, ncols // BLOCK, BLOCK * BLOCK), jnp.float32)
    grid = grid.at[:, :, band].set(values)
    grid = grid.reshape(nrows // BLOCK, ncols // BLOCK, BLOCK, BLOCK)
    blocks = jnp.einsum('ui,abuv,vj->aibj', table, grid, table, precision=lax.Precision.HIGHEST)
    return blocks.reshape(nrows, ncols)

def reference(activations, cotangent, momentum, band):
    table = cosine_table(BLOCK)

    def one_replica(rep_index):

        def add_group(group, total):
            start = ((rep_index * N_FSDP + group) * TOK_DEV).astype(jnp.int32)
            rows_in = lax.dynamic_slice_in_dim(activations, start, TOK_DEV, 0)
            rows_out = lax.dynamic_slice_in_dim(cotangent, start, TOK_DEV, 0)
            term = lax.dot_general(rows_in, rows_out, (((0,), (0,)), ((), ())), preferred_element_type=jnp.float32)
            rounded = lax.optimization_barrier(term.astype(jnp.bfloat16))
            return total + rounded.astype(jnp.float32)
        gradient = lax.fori_loop(0, N_FSDP, add_group, jnp.zeros((D, KV), jnp.float32))
        updated = DECAY * momentum[rep_index] + gradient
        values = forward_band(updated, table, band)
        fresh = updated - inverse_band(values, table, band, D, KV)
        return (fresh, values)
    fresh_all, values_all = lax.map(one_replica, jnp.arange(N_REP, dtype=jnp.int32))
    summed = lax.optimization_barrier(jnp.sum(values_all, axis=0))
    scale = BLOCK / math.sqrt(BAND * REPLICAS)
    update = (inverse_band(summed, table, band, D, KV) * scale).astype(jnp.bfloat16)
    return (fresh_all, update)
```

```python
import functools
import math

import jax
import jax.numpy as jnp
import numpy as np
from jax import lax
from jax.experimental import pallas as pl
from jax.experimental.pallas import tpu as pltpu
from jax.sharding import PartitionSpec as P

BLOCK = 64
BAND = 32
LOW = 16
DECAY = 0.9
ROWS = 256
HALVES = (((1, 2), (0, 3), (1, 2, 0, 3)), ((3, 2), (0, 1), (3, 2, 0, 1)))
X_MASKS = (4, 12)
Z_MASKS = (1, 3)
CHUNKS = {"a1": (True, 0, 256), "a2": (True, 512, 128), "b": (False, 768, 128)}
HIGHEST = lax.Precision.HIGHEST
VMEM = 32 * 1024 * 1024


def low_table():
    freq = np.arange(LOW, dtype=np.float64)[:, None]
    place = np.arange(BLOCK, dtype=np.float64)[None, :]
    factor = np.where(freq == 0, math.sqrt(1.0 / BLOCK), math.sqrt(2.0 / BLOCK))
    table = factor * np.cos(math.pi * (2.0 * place + 1.0) * freq / (2.0 * BLOCK))
    return np.kron(np.eye(ROWS // BLOCK), table).astype(np.float32)


def swap(value, axis, mask):
    n = lax.axis_size(axis)
    return lax.ppermute(value, axis, [(i, i ^ mask) for i in range(n)])


def targets_of(chunk, part):
    x_first = CHUNKS[chunk][0]
    steps = {ka: [] for ka in range(4)}
    for half, (sends, keeps, second) in enumerate(HALVES):
        for i, k1 in enumerate(sends if part == "send" else keeps):
            for j, k2 in enumerate(second):
                ka, kb = (k1, k2) if x_first else (k2, k1)
                steps[ka].append((half, i, j, kb))
    return steps


def term_kernel(jobs, first, pos_ref, act_ref, *refs):
    n_gt = first["n_gt"]
    gts = refs[:n_gt]
    outs = refs[n_gt:]
    step = pl.program_id(0)
    if first["transpose"] is not None:
        gt_out = outs[-1]
        col0, ncol = first["transpose"]

        @pl.when(step == 0)
        def _():
            gt_out[...] = gts[0][...].T

        gts = (gt_out,)
    for at, job in enumerate(jobs):

        @pl.when(step == at)
        def _(job=job):
            for gt, row, rows, out, i, j, kb in job:
                offset = pl.multiple_of((pos_ref[0] ^ kb) * ROWS, ROWS)
                block = act_ref[:, pl.ds(offset, ROWS)]
                outs[out][i, j] = jnp.dot(
                    gts[gt][row : row + rows, :], block, preferred_element_type=jnp.float32
                ).astype(jnp.bfloat16)


def position(order):
    me = lax.axis_index("fsdp")
    a, b = me // 4, me % 4
    return jnp.stack([b] + [a ^ k for k in order]).astype(jnp.int32)


def terms_to_send(activations, cotangent, chunk):
    _, col, half_cols = CHUNKS[chunk]
    tokens = activations.shape[0]
    steps = targets_of(chunk, "send")
    order = [k for k in (2, 1, 3, 0) if steps[k]]
    jobs = [[(0, h * half_cols, half_cols, h, i, j, kb) for h, i, j, kb in steps[k]] for k in order]
    ncol = 2 * half_cols
    block = jax.ShapeDtypeStruct((2, 4, half_cols, ROWS), jnp.bfloat16)
    whole = pl.BlockSpec((2, 4, half_cols, ROWS), lambda s, p: (0, 0, 0, 0))
    return pl.pallas_call(
        functools.partial(term_kernel, jobs, dict(n_gt=1, transpose=(col, ncol))),
        grid_spec=pltpu.PrefetchScalarGridSpec(
            num_scalar_prefetch=1,
            grid=(len(order),),
            in_specs=[
                pl.BlockSpec((tokens, 4 * ROWS), lambda s, p: (0, p[1 + s])),
                pl.BlockSpec((tokens, ncol), lambda s, p: (0, col // ncol)),
            ],
            out_specs=[whole, whole, pl.BlockSpec((ncol, tokens), lambda s, p: (0, 0))],
        ),
        out_shape=[block, block, jax.ShapeDtypeStruct((ncol, tokens), jnp.bfloat16)],
        compiler_params=pltpu.CompilerParams(vmem_limit_bytes=VMEM),
        cost_estimate=pl.CostEstimate(
            flops=16 * half_cols * ROWS * tokens * 2, bytes_accessed=tokens * 4096 * 2, transcendentals=0
        ),
        name="terms_" + chunk,
    )(position(order), activations, cotangent)


def terms_to_keep(activations, gts, chunks):
    tokens = activations.shape[0]
    order = [0, 1, 3, 2]
    jobs = [[] for _ in order]
    out_shape, out_specs = [], []
    for at, chunk in enumerate(chunks):
        half_cols = CHUNKS[chunk][2]
        steps = targets_of(chunk, "keep")
        for s, k in enumerate(order):
            jobs[s] += [(at, h * half_cols, half_cols, 2 * at + h, i, j, kb) for h, i, j, kb in steps[k]]
        out_shape += [jax.ShapeDtypeStruct((2, 4, half_cols, ROWS), jnp.bfloat16)] * 2
        out_specs += [pl.BlockSpec((2, 4, half_cols, ROWS), lambda s, p: (0, 0, 0, 0))] * 2
    used = [s for s in range(4) if jobs[s]]
    order, jobs = [order[s] for s in used], [jobs[s] for s in used]
    outs = pl.pallas_call(
        functools.partial(term_kernel, jobs, dict(n_gt=len(chunks), transpose=None)),
        grid_spec=pltpu.PrefetchScalarGridSpec(
            num_scalar_prefetch=1,
            grid=(len(order),),
            in_specs=[pl.BlockSpec((tokens, 4 * ROWS), lambda s, p: (0, p[1 + s]))]
            + [pl.BlockSpec(g.shape, lambda s, p: (0, 0)) for g in gts],
            out_specs=out_specs,
        ),
        out_shape=out_shape,
        compiler_params=pltpu.CompilerParams(vmem_limit_bytes=VMEM),
        cost_estimate=pl.CostEstimate(
            flops=sum(j[2] for job in jobs for j in job) * ROWS * tokens * 2,
            bytes_accessed=tokens * 4096 * 2,
            transcendentals=0,
        ),
        name="terms_keep_" + "_".join(chunks),
    )(position(order), activations, *gts)
    return {c: (outs[2 * i], outs[2 * i + 1]) for i, c in enumerate(chunks)}


def f32(x):
    return x.astype(jnp.float32)


def dot(a, b, dims=((1,), (0,))):
    return lax.dot_general(a, b, (dims, ((), ())), precision=HIGHEST, preferred_element_type=jnp.float32)


def final_kernel(half_cols, first_call, *refs):
    pieces = refs[:10]
    mom_ref, mask_ref, low_ref = refs[10:13]
    fresh_ref, coeff_ref = refs[13:] if first_call else refs[14:]
    halves = []
    for h in range(2):
        k, r, q, rz, qz = (ref[...].reshape(half_cols, ROWS) for ref in pieces[5 * h : 5 * h + 5])
        halves.append(f32(k) + f32(r) + f32(q) + f32(rz) + f32(qz))
    gradient = jnp.concatenate(halves, axis=0)
    low = low_ref[...]
    mask = mask_ref[...]
    for g in range(2 * half_cols // ROWS):
        cols = slice(g * ROWS, (g + 1) * ROWS)
        updated = DECAY * mom_ref[0, :, cols] + gradient[cols, :].T
        coeff = dot(dot(low, updated), low, ((1,), (1,))) * mask
        coeff_ref[g] = coeff
        fresh_ref[0, :, cols] = updated - dot(dot(low, coeff, ((0,), (0,))), low)


def finish(pieces, momentum, mask, low, chunk, fresh):
    _, col, half_cols = CHUNKS[chunk]
    ncol = 2 * half_cols
    groups = ncol // ROWS
    specs = []
    for _ in range(2):
        specs += [
            pl.BlockSpec((1, 1, half_cols, ROWS), lambda s: (0, 2, 0, 0)),
            pl.BlockSpec((1, 1, half_cols, ROWS), lambda s: (0, 2, 0, 0)),
            pl.BlockSpec((1, half_cols, ROWS), lambda s: (2, 0, 0)),
            pl.BlockSpec((1, half_cols, ROWS), lambda s: (0, 0, 0)),
            pl.BlockSpec((half_cols, ROWS), lambda s: (0, 0)),
        ]
    columns = pl.BlockSpec((1, ROWS, ncol), lambda s: (0, 0, col // ncol))
    specs += [columns, pl.BlockSpec((64, 64), lambda s: (0, 0)), pl.BlockSpec((64, ROWS), lambda s: (0, 0))]
    args = [*pieces[0], *pieces[1], momentum, mask, low]
    aliases = {}
    if fresh is not None:
        specs.append(pl.BlockSpec(memory_space=pl.ANY))
        args.append(fresh)
        aliases = {13: 0}
    return pl.pallas_call(
        functools.partial(final_kernel, half_cols, fresh is None),
        grid=(1,),
        in_specs=specs,
        out_specs=[columns, pl.BlockSpec((groups, 64, 64), lambda s: (0, 0, 0))],
        out_shape=[
            jax.ShapeDtypeStruct(momentum.shape, jnp.float32),
            jax.ShapeDtypeStruct((groups, 64, 64), jnp.float32),
        ],
        input_output_aliases=aliases,
        compiler_params=pltpu.CompilerParams(vmem_limit_bytes=VMEM),
        cost_estimate=pl.CostEstimate(flops=ncol * 1000000, bytes_accessed=ncol * 256 * 16, transcendentals=0),
        name="finish_" + chunk,
    )(*args)


def update_kernel(scale, parts, *refs):
    low_ref, out_ref = refs[-2:]
    low = low_ref[...]
    g = 0
    for ref, n in zip(refs[:-2], parts):
        for i in range(n):
            value = dot(dot(low, ref[i], ((0,), (0,))), low) * scale
            out_ref[:, g * ROWS : (g + 1) * ROWS] = value.astype(jnp.bfloat16)
            g += 1


def make_update(sums, low, ncols, scale):
    return pl.pallas_call(
        functools.partial(update_kernel, scale, [s.shape[0] for s in sums]),
        out_shape=jax.ShapeDtypeStruct((ROWS, ncols), jnp.bfloat16),
        compiler_params=pltpu.CompilerParams(vmem_limit_bytes=VMEM),
        name="update",
    )(*sums, low)


def per_device(activations, cotangent, momentum, band):
    low = jnp.asarray(low_table())
    spots = jnp.arange(LOW)[:, None] * BLOCK + jnp.arange(LOW)[None, :]
    chosen = (spots[:, :, None] == band[None, None, :]).any(axis=-1).astype(jnp.float32)
    mask = jnp.tile(chosen, (4, 4))

    sends, gts = {}, {}
    for c in ("a1", "b", "a2"):
        s1, s2, gts[c] = terms_to_send(activations, cotangent, c)
        sends[c] = (s1, s2)
    keeps = terms_to_keep(activations, [gts[c] for c in ("a1", "b", "a2")], ("a1", "b", "a2"))

    def masks(c):
        return (X_MASKS, Z_MASKS) if CHUNKS[c][0] else (Z_MASKS, X_MASKS)

    def chunk_flow(c):
        (m1, m2), (n1, n2) = masks(c)
        k = keeps[c]
        r = (swap(sends[c][0], "fsdp", m1), swap(sends[c][1], "fsdp", m2))
        t = [(f32(k[h][1]) + f32(r[h][1])).astype(jnp.bfloat16) for h in range(2)]
        q = (swap(t[0], "fsdp", m2), swap(t[1], "fsdp", m1))

        def total(h, j):
            return f32(k[h][0, j]) + f32(r[h][0, j]) + f32(q[h][j])

        v = [total(h, slice(0, 2)).astype(jnp.bfloat16) for h in range(2)]
        rz = (swap(v[0], "fsdp", n1), swap(v[1], "fsdp", n2))
        w = [(total(h, 3) + f32(rz[h][1])).astype(jnp.bfloat16) for h in range(2)]
        qz = (swap(w[0], "fsdp", n2), swap(w[1], "fsdp", n1))
        return [(k[h], r[h], q[h], rz[h], qz[h]) for h in range(2)]

    fresh = None
    coeffs = {}
    for c in ("b", "a1", "a2"):
        fresh, coeffs[c] = finish(chunk_flow(c), momentum, mask, low, c, fresh)
    summed = jnp.concatenate([coeffs[c] for c in ("a1", "a2", "b")], axis=0)
    for m in (1, 8, 2, 6):
        summed = summed + swap(summed, "rep", m)
    scale = BLOCK / math.sqrt(BAND * lax.axis_size("rep"))
    update = make_update([summed], low, momentum.shape[2], scale)
    return (fresh, update)


def solution(mesh):
    in_specs = (P(("rep", "fsdp"), None), P(("rep", "fsdp"), None), P("rep", "fsdp", None), P())
    out_specs = (P("rep", "fsdp", None), P("fsdp", None))
    return jax.shard_map(
        per_device, mesh=mesh, in_specs=in_specs, out_specs=out_specs, check_vma=False
    )
```

```python
import functools
import math

import jax
import jax.numpy as jnp
import numpy as np
from jax import lax
from jax.experimental import pallas as pl
from jax.experimental.pallas import tpu as pltpu
from jax.sharding import PartitionSpec as P

BLOCK = 64
BAND = 32
LOW = 16
DECAY = 0.9
ROWS = 256
CHAINS = (
    (192, (3, 4, 12, 1)),
    (256, (12, 4, 1, 3)),
    (256, (4, 12, 3, 1)),
    (192, (1, 12, 3, 4)),
    (128, (4, 1, 12, 3)),
)
SCHEDULE = (
    (2, 0), (1, 0), (3, 0), (0, 0), (4, 0), (2, 1), (1, 1), (4, 1), (3, 1), (2, 2),
    (0, 1), (1, 2), (3, 2), (4, 2), (0, 2), (2, 3), (4, 3), (1, 3), (0, 3), (3, 3),
)
VMEM = 40 * 1024 * 1024
TERMS_VMEM = 40 * 1024 * 1024
IN_VMEM = pl.BlockSpec(memory_space=pltpu.VMEM)


def low_table():
    freq = np.arange(LOW, dtype=np.float64)[:, None]
    place = np.arange(BLOCK, dtype=np.float64)[None, :]
    factor = np.where(freq == 0, math.sqrt(1.0 / BLOCK), math.sqrt(2.0 / BLOCK))
    table = factor * np.cos(math.pi * (2.0 * place + 1.0) * freq / (2.0 * BLOCK))
    whole = np.kron(np.eye(ROWS // BLOCK), table).astype(np.float32)
    first = whole.astype(jnp.bfloat16)
    second = (whole - first.astype(np.float32)).astype(jnp.bfloat16)
    return np.concatenate([first, second], axis=0)


def swap(value, axis, mask):
    n = lax.axis_size(axis)
    return lax.ppermute(value, axis, [(i, i ^ mask) for i in range(n)])


def digits(offset, masks):
    for index in range(16):
        bits = [(index >> (3 - i)) & 1 for i in range(4)]
        if functools.reduce(lambda a, b: a ^ b, [m * b for m, b in zip(masks, bits)]) == offset:
            return index
    raise ValueError(offset)


def terms_kernel(pos_ref, act_ref, cot_ref, *refs):
    outs = refs[: 2 * len(CHAINS)]
    gt_ref, buf_ref, cot_buf, sem_ref = refs[2 * len(CHAINS) :]
    a, b = pos_ref[0], pos_ref[1]
    width = buf_ref.shape[2]

    def load(ka):
        start = pl.multiple_of((a ^ ka) * width, width)
        return pltpu.make_async_copy(act_ref.at[:, pl.ds(start, width)], buf_ref.at[ka], sem_ref.at[ka])

    cot_copy = pltpu.make_async_copy(cot_ref, cot_buf, sem_ref.at[4])
    cot_copy.start()
    for ka in range(4):
        load(ka).start()
    cot_copy.wait()
    gt_ref[...] = cot_buf[...].T
    for ka in range(4):
        load(ka).wait()
        for kb in range(4):
            offset = pl.multiple_of((b ^ kb) * ROWS, ROWS)
            product = jnp.dot(
                gt_ref[...], buf_ref[ka, :, pl.ds(offset, ROWS)], preferred_element_type=jnp.float32
            ).astype(jnp.bfloat16)
            row = 0
            for c, (ncol, masks) in enumerate(CHAINS):
                index = digits(4 * ka + kb, masks)
                outs[2 * c + (0 if index >= 8 else 1)][index % 8] = product[row : row + ncol]
                row += ncol


def terms(activations, cotangent, pos):
    tokens, width = activations.shape
    shapes = [jax.ShapeDtypeStruct((8, n, ROWS), jnp.bfloat16) for n, _ in CHAINS for _ in range(2)]
    return pl.pallas_call(
        terms_kernel,
        in_specs=[
            pl.BlockSpec(memory_space=pltpu.SMEM),
            pl.BlockSpec(memory_space=pltpu.HBM),
            pl.BlockSpec(memory_space=pltpu.HBM),
        ],
        out_specs=[IN_VMEM] * len(shapes),
        out_shape=shapes,
        scratch_shapes=[
            pltpu.VMEM((cotangent.shape[1], tokens), jnp.bfloat16),
            pltpu.VMEM((4, tokens, width // 4), jnp.bfloat16),
            pltpu.VMEM(cotangent.shape, jnp.bfloat16),
            pltpu.SemaphoreType.DMA((5,)),
        ],
        compiler_params=pltpu.CompilerParams(vmem_limit_bytes=TERMS_VMEM),
        cost_estimate=pl.CostEstimate(
            flops=2 * tokens * width * cotangent.shape[1], bytes_accessed=tokens * width * 2, transcendentals=0
        ),
        name="terms",
    )(pos, activations, cotangent)


def f32(x):
    return x.astype(jnp.float32)


def dot(a, b, dims=((1,), (0,))):
    return lax.dot_general(a, b, (dims, ((), ())), preferred_element_type=jnp.float32)


def split(x):
    first = x.astype(jnp.bfloat16)
    return first, (x - f32(first)).astype(jnp.bfloat16)


def forward(matrix, low):
    first, second = split(matrix)
    both = dot(low, first)
    left = both[:64] + both[64:] + dot(low[:64], second)
    stacked = jnp.concatenate([left[:, c : c + ROWS] for c in range(0, left.shape[1], ROWS)], axis=0)
    first, second = split(stacked)
    both = dot(first, low, ((1,), (1,)))
    return both[:, :64] + both[:, 64:] + dot(second, low[:64], ((1,), (1,)))


def backward(coeff, low):
    first, second = split(coeff)
    right = dot(first, low[:64]) + dot(first, low[64:]) + dot(second, low[:64])
    beside = jnp.concatenate([right[r : r + 64] for r in range(0, right.shape[0], 64)], axis=1)
    first, second = split(beside)
    three = jnp.concatenate([low, low[:64]], axis=0)
    return dot(three, jnp.concatenate([first, first, second], axis=0), ((0,), (0,)))


def add_kernel(size, *refs):
    for i in range(size):
        parts = [f32(ref[size + i]) for ref in refs[:-1]]
        refs[-1][i] = functools.reduce(jnp.add, parts).astype(jnp.bfloat16)


def add(held, size, name):
    _, rows, cols = held[0].shape
    return pl.pallas_call(
        functools.partial(add_kernel, size),
        in_specs=[IN_VMEM] * len(held),
        out_specs=IN_VMEM,
        out_shape=jax.ShapeDtypeStruct((size, rows, cols), jnp.bfloat16),
        compiler_params=pltpu.CompilerParams(vmem_limit_bytes=VMEM),
        cost_estimate=pl.CostEstimate(flops=size * 100000, bytes_accessed=size * rows * 512 * 3, transcendentals=0),
        name=name,
    )(*held)


def coeff_kernel(counts, *refs):
    n = sum(counts)
    mom_ref, band_ref, low_ref, updated_ref, coeff_ref = refs[n:]
    row = lax.broadcasted_iota(jnp.int32, (64, 64), 0) % LOW
    spot = row * BLOCK + lax.broadcasted_iota(jnp.int32, (64, 64), 1) % LOW
    chosen = functools.reduce(jnp.logical_or, [spot == band_ref[i] for i in range(BAND)])
    mask = chosen.astype(jnp.float32)
    rows, at = [], 0
    for count in counts:
        parts = [f32(ref[0]) for ref in refs[at : at + count]]
        rows.append(functools.reduce(jnp.add, parts))
        at += count
    gradient = jnp.concatenate(rows, axis=0)
    turned = [gradient[c : c + ROWS].T for c in range(0, gradient.shape[0], ROWS)]
    updated = DECAY * mom_ref[0] + jnp.concatenate(turned, axis=1)
    updated_ref[...] = updated
    coeff_ref[...] = forward(updated, low_ref[...]) * jnp.concatenate([mask] * len(turned), axis=0)


def coefficients(held, momentum, band, low):
    _, rows, ncol = momentum.shape
    arrays = [a for chain in held for a in chain]
    return pl.pallas_call(
        functools.partial(coeff_kernel, [len(chain) for chain in held]),
        in_specs=[IN_VMEM] * (len(arrays) + 1) + [pl.BlockSpec(memory_space=pltpu.SMEM), IN_VMEM],
        out_specs=[IN_VMEM] * 2,
        out_shape=[
            jax.ShapeDtypeStruct((rows, ncol), jnp.float32),
            jax.ShapeDtypeStruct((ncol // 4, 64), jnp.float32),
        ],
        compiler_params=pltpu.CompilerParams(vmem_limit_bytes=VMEM),
        cost_estimate=pl.CostEstimate(flops=ncol * 1000000, bytes_accessed=ncol * 256 * 8, transcendentals=0),
        name="coefficients",
    )(*arrays, momentum, band, low)


def fresh_kernel(updated_ref, coeff_ref, low_ref, out_ref):
    out_ref[0] = updated_ref[...] - backward(coeff_ref[...], low_ref[...])


def new_momentum(updated, coeffs, low, shape):
    return pl.pallas_call(
        fresh_kernel,
        in_specs=[IN_VMEM] * 3,
        out_shape=jax.ShapeDtypeStruct(shape, jnp.float32),
        compiler_params=pltpu.CompilerParams(vmem_limit_bytes=VMEM),
        cost_estimate=pl.CostEstimate(flops=2000000000, bytes_accessed=2000000, transcendentals=0),
        name="new_momentum",
    )(updated, coeffs, low)


def update_kernel(scale, a_ref, b_ref, c_ref, d_ref, low_ref, out_ref):
    total = (a_ref[...] + b_ref[...]) + (c_ref[...] + d_ref[...])
    out_ref[...] = (backward(total, low_ref[...]) * scale).astype(jnp.bfloat16)


def make_update(parts, low, ncols, scale):
    return pl.pallas_call(
        functools.partial(update_kernel, scale),
        in_specs=[IN_VMEM] * 5,
        out_shape=jax.ShapeDtypeStruct((ROWS, ncols), jnp.bfloat16),
        compiler_params=pltpu.CompilerParams(vmem_limit_bytes=VMEM),
        name="update",
    )(*parts, low)


def per_device(activations, cotangent, momentum, band):
    low = jnp.asarray(low_table())
    me = lax.axis_index("fsdp")
    blocks = terms(activations, cotangent, jnp.stack([me >> 2, me & 3]).astype(jnp.int32))

    held = [[blocks[2 * c + 1]] for c in range(len(CHAINS))]
    before = blocks[0]
    for c, stage in SCHEDULE:
        if stage:
            held[c][-1], before = lax.optimization_barrier((held[c][-1], before))
            send = add(held[c], 8 >> stage, "add%d_%d" % (c, stage))
        else:
            send, before = lax.optimization_barrier((blocks[2 * c], before))
        held[c].append(swap(send, "fsdp", CHAINS[c][1][stage]))
        before = send

    updated, coeffs = coefficients(held, momentum, band, low)
    fresh = new_momentum(updated, coeffs, low, momentum.shape)
    summed = coeffs
    for m in (1, 8):
        summed = summed + swap(summed, "rep", m)
    parts = [summed] + [swap(summed, "rep", m) for m in (2, 4, 6)]
    scale = BLOCK / math.sqrt(BAND * lax.axis_size("rep"))
    update = make_update(parts, low, momentum.shape[2], scale)
    return (fresh, update)


def solution(mesh):
    in_specs = (P(("rep", "fsdp"), None), P(("rep", "fsdp"), None), P("rep", "fsdp", None), P())
    out_specs = (P("rep", "fsdp", None), P("fsdp", None))
    return jax.shard_map(
        per_device, mesh=mesh, in_specs=in_specs, out_specs=out_specs, check_vma=False
    )
```

```python
import functools
import math

import jax
import jax.numpy as jnp
import numpy as np
from jax import lax
from jax.experimental import pallas as pl
from jax.experimental.pallas import tpu as pltpu
from jax.sharding import PartitionSpec as P

BLOCK = 64
BAND = 32
LOW = 16
DECAY = 0.9
ROWS = 256
CHAINS = (
    (256, (12, 4, 1, 3)),
    (128, (4, 12, 1, 3)),
    (192, (3, 12, 4, 1)),
    (192, (1, 4, 3, 12)),
    (256, (4, 12, 3, 1)),
)
SCHEDULE = (
    (4, 0), (2, 0), (3, 0), (0, 0), (4, 1), (0, 1), (2, 1), (1, 0), (1, 1), (3, 1),
    (4, 2), (0, 2), (2, 2), (3, 2), (4, 3), (1, 2), (2, 3), (0, 3), (1, 3), (3, 3),
)
VMEM = 40 * 1024 * 1024
TERMS_VMEM = 50 * 1024 * 1024
IN_VMEM = pl.BlockSpec(memory_space=pltpu.VMEM)


def low_table():
    freq = np.arange(LOW, dtype=np.float64)[:, None]
    place = np.arange(BLOCK, dtype=np.float64)[None, :]
    factor = np.where(freq == 0, math.sqrt(1.0 / BLOCK), math.sqrt(2.0 / BLOCK))
    table = factor * np.cos(math.pi * (2.0 * place + 1.0) * freq / (2.0 * BLOCK))
    whole = np.kron(np.eye(ROWS // BLOCK), table).astype(np.float32)
    first = whole.astype(jnp.bfloat16)
    second = (whole - first.astype(np.float32)).astype(jnp.bfloat16)
    return np.concatenate([first, second], axis=0)


def swap(value, axis, mask):
    n = lax.axis_size(axis)
    return lax.ppermute(value, axis, [(i, i ^ mask) for i in range(n)])


def digits(offset, masks):
    for index in range(16):
        bits = [(index >> (3 - i)) & 1 for i in range(4)]
        if functools.reduce(lambda a, b: a ^ b, [m * b for m, b in zip(masks, bits)]) == offset:
            return index
    raise ValueError(offset)


def terms_kernel(kept, pos_ref, act_ref, cot_ref, *refs):
    outs = refs[: len(CHAINS)]
    gt_ref, buf_ref, cot_buf, sem_ref = refs[len(CHAINS) :]
    a, b = pos_ref[0], pos_ref[1]
    width = buf_ref.shape[2]
    order = (0, 3, 1, 2) if kept else (2, 1, 3, 0)

    def load(ka):
        start = pl.multiple_of((a ^ ka) * width, width)
        return pltpu.make_async_copy(act_ref.at[:, pl.ds(start, width)], buf_ref.at[ka], sem_ref.at[ka])

    cot_copy = pltpu.make_async_copy(cot_ref, cot_buf, sem_ref.at[4])
    cot_copy.start()
    for ka in order:
        load(ka).start()
    cot_copy.wait()
    gt_ref[...] = cot_buf[...].T
    for ka in order:
        load(ka).wait()
        for kb in range(4):
            offset = pl.multiple_of((b ^ kb) * ROWS, ROWS)
            runs, row = [], 0
            for c, (ncol, masks) in enumerate(CHAINS):
                index = digits(4 * ka + kb, masks)
                if (index < 8) == kept:
                    if runs and runs[-1][1] == row:
                        runs[-1][1] += ncol
                    else:
                        runs.append([row, row + ncol, []])
                    runs[-1][2].append((c, index % 8, ncol))
                row += ncol
            for first, last, members in runs:
                product = jnp.dot(
                    gt_ref[first:last, :], buf_ref[ka, :, pl.ds(offset, ROWS)], preferred_element_type=jnp.float32
                ).astype(jnp.bfloat16)
                at = 0
                for c, index, ncol in members:
                    outs[c][index] = product[at : at + ncol]
                    at += ncol


def terms(activations, cotangent, pos, kept):
    tokens, width = activations.shape
    shapes = [jax.ShapeDtypeStruct((8, n, ROWS), jnp.bfloat16) for n, _ in CHAINS]
    return pl.pallas_call(
        functools.partial(terms_kernel, kept),
        in_specs=[
            pl.BlockSpec(memory_space=pltpu.SMEM),
            pl.BlockSpec(memory_space=pltpu.HBM),
            pl.BlockSpec(memory_space=pltpu.HBM),
        ],
        out_specs=[IN_VMEM] * len(shapes),
        out_shape=shapes,
        scratch_shapes=[
            pltpu.VMEM((cotangent.shape[1], tokens), jnp.bfloat16),
            pltpu.VMEM((4, tokens, width // 4), jnp.bfloat16),
            pltpu.VMEM(cotangent.shape, jnp.bfloat16),
            pltpu.SemaphoreType.DMA((5,)),
        ],
        compiler_params=pltpu.CompilerParams(vmem_limit_bytes=(46 if kept else 50) * 2**20),
        cost_estimate=pl.CostEstimate(
            flops=tokens * width * cotangent.shape[1], bytes_accessed=tokens * width * 2, transcendentals=0
        ),
        name="terms_kept" if kept else "terms_sent",
    )(pos, activations, cotangent)


def f32(x):
    return x.astype(jnp.float32)


def dot(a, b, dims=((1,), (0,))):
    return lax.dot_general(a, b, (dims, ((), ())), preferred_element_type=jnp.float32)


def split(x):
    first = x.astype(jnp.bfloat16)
    return first, (x - f32(first)).astype(jnp.bfloat16)


def forward(matrix, low):
    first, second = split(matrix)
    both = dot(low, first)
    left = both[:64] + both[64:] + dot(low[:64], second)
    stacked = jnp.concatenate([left[:, c : c + ROWS] for c in range(0, left.shape[1], ROWS)], axis=0)
    first, second = split(stacked)
    both = dot(first, low, ((1,), (1,)))
    coeff = both[:, :64] + both[:, 64:] + dot(second, low[:64], ((1,), (1,)))
    half = coeff.shape[0] // 2
    return jnp.concatenate([coeff[:half], coeff[half:]], axis=1)


def backward(coeff, low):
    first, second = split(jnp.concatenate([coeff[:, :64], coeff[:, 64:]], axis=0))
    right = dot(first, low[:64]) + dot(first, low[64:]) + dot(second, low[:64])
    beside = jnp.concatenate([right[r : r + 64] for r in range(0, right.shape[0], 64)], axis=1)
    first, second = split(beside)
    three = jnp.concatenate([low, low[:64]], axis=0)
    return dot(three, jnp.concatenate([first, first, second], axis=0), ((0,), (0,)))


def add_kernel(size, *refs):
    for i in range(size):
        parts = [f32(ref[size + i]) for ref in refs[:-1]]
        refs[-1][i] = functools.reduce(jnp.add, parts).astype(jnp.bfloat16)


def add(held, size, name):
    _, rows, cols = held[0].shape
    return pl.pallas_call(
        functools.partial(add_kernel, size),
        in_specs=[IN_VMEM] * len(held),
        out_specs=IN_VMEM,
        out_shape=jax.ShapeDtypeStruct((size, rows, cols), jnp.bfloat16),
        compiler_params=pltpu.CompilerParams(vmem_limit_bytes=VMEM),
        cost_estimate=pl.CostEstimate(flops=size, bytes_accessed=size, transcendentals=0),
        name=name,
    )(*held)


def coeff_kernel(counts, *refs):
    n = sum(counts)
    mom_ref, band_ref, low_ref, updated_ref, coeff_ref = refs[n:]
    row = lax.broadcasted_iota(jnp.int32, coeff_ref.shape, 0) % LOW
    spot = row * BLOCK + lax.broadcasted_iota(jnp.int32, coeff_ref.shape, 1) % LOW
    chosen = functools.reduce(jnp.logical_or, [spot == band_ref[i] for i in range(BAND)])
    mask = chosen.astype(jnp.float32)
    rows, at = [], 0
    for count in counts:
        parts = [f32(ref[0]) for ref in refs[at : at + count]]
        rows.append(functools.reduce(jnp.add, parts))
        at += count
    gradient = jnp.concatenate(rows, axis=0)
    turned = [gradient[c : c + ROWS].T for c in range(0, gradient.shape[0], ROWS)]
    updated = DECAY * mom_ref[0] + jnp.concatenate(turned, axis=1)
    updated_ref[...] = updated
    coeff_ref[...] = forward(updated, low_ref[...]) * mask


def coefficients(held, momentum, band, low):
    _, rows, ncol = momentum.shape
    arrays = [a for chain in held for a in chain]
    return pl.pallas_call(
        functools.partial(coeff_kernel, [len(chain) for chain in held]),
        in_specs=[IN_VMEM] * (len(arrays) + 1) + [pl.BlockSpec(memory_space=pltpu.SMEM), IN_VMEM],
        out_specs=[IN_VMEM] * 2,
        out_shape=[
            jax.ShapeDtypeStruct((rows, ncol), jnp.float32),
            jax.ShapeDtypeStruct((ncol // 8, 128), jnp.float32),
        ],
        compiler_params=pltpu.CompilerParams(vmem_limit_bytes=VMEM),
        cost_estimate=pl.CostEstimate(flops=ncol * 1000000, bytes_accessed=ncol * 256 * 8, transcendentals=0),
        name="coefficients",
    )(*arrays, momentum, band, low)


def fresh_kernel(updated_ref, coeff_ref, low_ref, out_ref):
    out_ref[0] = updated_ref[...] - backward(coeff_ref[...], low_ref[...])


def new_momentum(updated, coeffs, low, shape):
    return pl.pallas_call(
        fresh_kernel,
        in_specs=[IN_VMEM] * 3,
        out_shape=jax.ShapeDtypeStruct(shape, jnp.float32),
        compiler_params=pltpu.CompilerParams(vmem_limit_bytes=VMEM),
        cost_estimate=pl.CostEstimate(flops=2000000000, bytes_accessed=2000000, transcendentals=0),
        name="new_momentum",
    )(updated, coeffs, low)


def update_kernel(scale, a_ref, b_ref, c_ref, d_ref, low_ref, out_ref):
    total = (a_ref[...] + b_ref[...]) + (c_ref[...] + d_ref[...])
    out_ref[...] = (backward(total, low_ref[...]) * scale).astype(jnp.bfloat16)


def make_update(parts, low, ncols, scale):
    return pl.pallas_call(
        functools.partial(update_kernel, scale),
        in_specs=[IN_VMEM] * 5,
        out_shape=jax.ShapeDtypeStruct((ROWS, ncols), jnp.bfloat16),
        compiler_params=pltpu.CompilerParams(vmem_limit_bytes=VMEM),
        name="update",
    )(*parts, low)


def per_device(activations, cotangent, momentum, band):
    low = jnp.asarray(low_table())
    me = lax.axis_index("fsdp")
    pos = jnp.stack([me >> 2, me & 3]).astype(jnp.int32)
    sent = terms(activations, cotangent, pos, False)
    pos, _ = lax.optimization_barrier((pos, sent[0]))
    kept = terms(activations, cotangent, pos, True)

    held = [[k] for k in kept]
    before = sent[0]
    for c, stage in SCHEDULE:
        if stage:
            held[c][-1], before = lax.optimization_barrier((held[c][-1], before))
            send = add(held[c], 8 >> stage, "add%d_%d" % (c, stage))
        else:
            send = sent[c]
        held[c].append(swap(send, "fsdp", CHAINS[c][1][stage]))
        before = send if stage else before

    updated, coeffs = coefficients(held, momentum, band, low)
    fresh = new_momentum(updated, coeffs, low, momentum.shape)
    summed = coeffs
    for m in (1, 8):
        summed = summed + swap(summed, "rep", m)
    parts = [summed] + [swap(summed, "rep", m) for m in (2, 4, 6)]
    scale = BLOCK / math.sqrt(BAND * lax.axis_size("rep"))
    update = make_update(parts, low, momentum.shape[2], scale)
    return (fresh, update)


def solution(mesh):
    in_specs = (P(("rep", "fsdp"), None), P(("rep", "fsdp"), None), P("rep", "fsdp", None), P())
    out_specs = (P("rep", "fsdp", None), P("fsdp", None))
    return jax.shard_map(
        per_device, mesh=mesh, in_specs=in_specs, out_specs=out_specs, check_vma=False
    )
```

```python
import functools
import math

import jax
import jax.numpy as jnp
import numpy as np
from jax import lax
from jax.experimental import pallas as pl
from jax.experimental.pallas import tpu as pltpu
from jax.sharding import PartitionSpec as P

BLOCK = 64
BAND = 32
LOW = 16
DECAY = 0.9
ROWS = 256
CHAINS = (
    (256, (12, 4, 1, 3)),
    (256, (4, 12, 3, 1)),
    (128, (4, 12, 1, 3)),
    (192, (3, 12, 4, 1)),
    (192, (1, 4, 3, 12)),
)
SCHEDULE = (
    (1, 0), (3, 0), (4, 0), (0, 0), (1, 1), (0, 1), (3, 1), (2, 0), (2, 1), (4, 1),
    (1, 2), (0, 2), (3, 2), (4, 2), (1, 3), (2, 2), (3, 3), (0, 3), (2, 3), (4, 3),
)
VMEM = 16 * 1024 * 1024
TERMS_VMEM = 50 * 1024 * 1024
IN_VMEM = pl.BlockSpec(memory_space=pltpu.VMEM)


def low_table():
    freq = np.arange(LOW, dtype=np.float64)[:, None]
    place = np.arange(BLOCK, dtype=np.float64)[None, :]
    factor = np.where(freq == 0, math.sqrt(1.0 / BLOCK), math.sqrt(2.0 / BLOCK))
    table = factor * np.cos(math.pi * (2.0 * place + 1.0) * freq / (2.0 * BLOCK))
    whole = np.kron(np.eye(ROWS // BLOCK), table).astype(np.float32)
    first = whole.astype(jnp.bfloat16)
    second = (whole - first.astype(np.float32)).astype(jnp.bfloat16)
    return np.concatenate([first, second], axis=0)


def swap(value, axis, mask):
    n = lax.axis_size(axis)
    return lax.ppermute(value, axis, [(i, i ^ mask) for i in range(n)])


def digits(offset, masks):
    for index in range(16):
        bits = [(index >> (3 - i)) & 1 for i in range(4)]
        if functools.reduce(lambda a, b: a ^ b, [m * b for m, b in zip(masks, bits)]) == offset:
            return index
    raise ValueError(offset)


def terms_kernel(kept, act_ref, cot_ref, *refs):
    outs = refs[: len(CHAINS)]
    gt_ref, buf_ref, cot_buf, sem_ref = refs[len(CHAINS) :]
    me = lax.axis_index("fsdp")
    a, b = me >> 2, me & 3
    width = buf_ref.shape[2]
    order = (0, 3, 1, 2) if kept else (2, 1, 3, 0)

    def load(ka):
        start = pl.multiple_of((a ^ ka) * width, width)
        return pltpu.make_async_copy(act_ref.at[:, pl.ds(start, width)], buf_ref.at[ka], sem_ref.at[ka])

    cot_copy = pltpu.make_async_copy(cot_ref, cot_buf, sem_ref.at[4])
    cot_copy.start()
    load(order[0]).start()
    cot_copy.wait()
    for ka in order[1:]:
        load(ka).start()
    gt_ref[...] = cot_buf[...].T
    for ka in order:
        load(ka).wait()
        for kb in range(4):
            offset = pl.multiple_of((b ^ kb) * ROWS, ROWS)
            runs, row = [], 0
            for c, (ncol, masks) in enumerate(CHAINS):
                index = digits(4 * ka + kb, masks)
                if (index < 8) == kept:
                    if runs and runs[-1][1] == row:
                        runs[-1][1] += ncol
                    else:
                        runs.append([row, row + ncol, []])
                    runs[-1][2].append((c, index % 8, ncol))
                row += ncol
            for first, last, members in runs:
                product = jnp.dot(
                    gt_ref[first:last, :], buf_ref[ka, :, pl.ds(offset, ROWS)], preferred_element_type=jnp.float32
                ).astype(jnp.bfloat16)
                at = 0
                for c, index, ncol in members:
                    outs[c][index] = product[at : at + ncol]
                    at += ncol


def terms(activations, cotangent, kept):
    tokens, width = activations.shape
    shapes = [jax.ShapeDtypeStruct((8, n, ROWS), jnp.bfloat16) for n, _ in CHAINS]
    return pl.pallas_call(
        functools.partial(terms_kernel, kept),
        in_specs=[
            pl.BlockSpec(memory_space=pltpu.HBM),
            pl.BlockSpec(memory_space=pltpu.HBM),
        ],
        out_specs=[IN_VMEM] * len(shapes),
        out_shape=shapes,
        scratch_shapes=[
            pltpu.VMEM((cotangent.shape[1], tokens), jnp.bfloat16),
            pltpu.VMEM((4, tokens, width // 4), jnp.bfloat16),
            pltpu.VMEM(cotangent.shape, jnp.bfloat16),
            pltpu.SemaphoreType.DMA((5,)),
        ],
        compiler_params=pltpu.CompilerParams(vmem_limit_bytes=(46 if kept else 50) * 2**20),
        cost_estimate=pl.CostEstimate(
            flops=tokens * width * cotangent.shape[1], bytes_accessed=tokens * width * 2, transcendentals=0
        ),
        name="terms_kept" if kept else "terms_sent",
    )(activations, cotangent)


def f32(x):
    return x.astype(jnp.float32)


def dot(a, b, dims=((1,), (0,))):
    return lax.dot_general(a, b, (dims, ((), ())), preferred_element_type=jnp.float32)


def split(x):
    first = x.astype(jnp.bfloat16)
    return first, (x - f32(first)).astype(jnp.bfloat16)


def forward(matrix, low):
    first, second = split(matrix)
    both = dot(low, first)
    left = both[:64] + both[64:] + dot(low[:64], second)
    stacked = jnp.concatenate([left[:, c : c + ROWS] for c in range(0, left.shape[1], ROWS)], axis=0)
    first, second = split(stacked)
    both = dot(first, low, ((1,), (1,)))
    return both[:, :64] + both[:, 64:] + dot(second, low[:64], ((1,), (1,)))


def backward(coeff, low):
    first, second = split(coeff)
    right = dot(first, low[:64]) + dot(first, low[64:]) + dot(second, low[:64])
    beside = jnp.concatenate([right[r : r + 64] for r in range(0, right.shape[0], 64)], axis=1)
    first, second = split(beside)
    three = jnp.concatenate([low, low[:64]], axis=0)
    return dot(three, jnp.concatenate([first, first, second], axis=0), ((0,), (0,)))


def add_kernel(size, *refs):
    for i in range(size):
        parts = [f32(ref[size + i]) for ref in refs[:-1]]
        refs[-1][i] = functools.reduce(jnp.add, parts).astype(jnp.bfloat16)


def add(held, size, name):
    _, rows, cols = held[0].shape
    return pl.pallas_call(
        functools.partial(add_kernel, size),
        in_specs=[IN_VMEM] * len(held),
        out_specs=IN_VMEM,
        out_shape=jax.ShapeDtypeStruct((size, rows, cols), jnp.bfloat16),
        compiler_params=pltpu.CompilerParams(vmem_limit_bytes=VMEM),
        cost_estimate=pl.CostEstimate(flops=size, bytes_accessed=size, transcendentals=0),
        name=name,
    )(*held)


def band_tables(band, rows):
    width = band.shape[1]
    column = lax.broadcasted_iota(jnp.int32, (64, width), 1) % 4 * LOW + band % BLOCK
    pick = (lax.broadcasted_iota(jnp.int32, (64, width), 0) == column).astype(jnp.bfloat16)
    keep = (lax.broadcasted_iota(jnp.int32, (rows, width), 0) % LOW == band // BLOCK).astype(jnp.float32)
    own = lax.broadcasted_iota(jnp.int32, (rows // LOW, rows), 1) // LOW
    gather = (own == lax.broadcasted_iota(jnp.int32, (rows // LOW, rows), 0)).astype(jnp.bfloat16)
    return pick, keep, gather


def both_of(x, table, dims=((1,), (0,))):
    first, second = split(x)
    return dot(first, table, dims) + dot(second, table, dims)


def coeff_kernel(counts, *refs):
    n = sum(counts)
    mom_ref, band_ref, low_ref, updated_ref, coeff_ref, chosen_ref = refs[n:]
    rows, at = [], 0
    for count in counts:
        parts = [f32(ref[0]) for ref in refs[at : at + count]]
        rows.append(functools.reduce(jnp.add, parts))
        at += count
    gradient = jnp.concatenate(rows, axis=0)
    turned = [gradient[c : c + ROWS].T for c in range(0, gradient.shape[0], ROWS)]
    updated = DECAY * mom_ref[0] + jnp.concatenate(turned, axis=1)
    updated_ref[...] = updated
    coeff = forward(updated, low_ref[...])
    pick, keep, gather = band_tables(band_ref[...], coeff.shape[0])
    picked = both_of(coeff, pick) * keep
    first, second = split(picked)
    chosen_ref[...] = dot(gather, first) + dot(gather, second)
    coeff_ref[...] = both_of(picked, pick, ((1,), (1,)))


def coefficients(held, momentum, band, low):
    _, rows, ncol = momentum.shape
    arrays = [a for chain in held for a in chain]
    return pl.pallas_call(
        functools.partial(coeff_kernel, [len(chain) for chain in held]),
        in_specs=[IN_VMEM] * (len(arrays) + 3),
        out_specs=[IN_VMEM] * 3,
        out_shape=[
            jax.ShapeDtypeStruct((rows, ncol), jnp.float32),
            jax.ShapeDtypeStruct((ncol // 4, 64), jnp.float32),
            jax.ShapeDtypeStruct((ncol // 64, 4 * BAND), jnp.float32),
        ],
        compiler_params=pltpu.CompilerParams(vmem_limit_bytes=VMEM),
        cost_estimate=pl.CostEstimate(flops=ncol * 1000000, bytes_accessed=ncol * 256 * 8, transcendentals=0),
        name="coefficients",
    )(*arrays, momentum, band, low)


def fresh_kernel(updated_ref, coeff_ref, low_ref, out_ref):
    out_ref[0] = updated_ref[...] - backward(coeff_ref[...], low_ref[...])


def new_momentum(updated, coeffs, low, shape):
    return pl.pallas_call(
        fresh_kernel,
        in_specs=[IN_VMEM] * 3,
        out_shape=jax.ShapeDtypeStruct(shape, jnp.float32),
        compiler_params=pltpu.CompilerParams(vmem_limit_bytes=VMEM),
        cost_estimate=pl.CostEstimate(flops=2000000000, bytes_accessed=2000000, transcendentals=0),
        name="new_momentum",
    )(updated, coeffs, low)


def update_kernel(scale, a_ref, b_ref, c_ref, d_ref, band_ref, low_ref, out_ref):
    total = (a_ref[...] + b_ref[...]) + (c_ref[...] + d_ref[...])
    pick, keep, gather = band_tables(band_ref[...], LOW * total.shape[0])
    first, second = split(total)
    spread = (dot(gather, first, ((0,), (0,))) + dot(gather, second, ((0,), (0,)))) * keep
    coeff = both_of(spread, pick, ((1,), (1,)))
    out_ref[...] = (backward(coeff, low_ref[...]) * scale).astype(jnp.bfloat16)


def make_update(parts, band, low, ncols, scale):
    return pl.pallas_call(
        functools.partial(update_kernel, scale),
        in_specs=[IN_VMEM] * 6,
        out_shape=jax.ShapeDtypeStruct((ROWS, ncols), jnp.bfloat16),
        compiler_params=pltpu.CompilerParams(vmem_limit_bytes=VMEM),
        name="update",
    )(*parts, band, low)


def per_device(activations, cotangent, momentum, band):
    low = jnp.asarray(low_table())
    sent = terms(activations, cotangent, False)
    cotangent, _ = lax.optimization_barrier((cotangent, sent[0]))
    kept = terms(activations, cotangent, True)
    held = [[k] for k in kept]
    before = sent[0]
    for c, stage in SCHEDULE:
        if stage:
            held[c][-1], before = lax.optimization_barrier((held[c][-1], before))
            send = add(held[c], 8 >> stage, "add%d_%d" % (c, stage))
        else:
            send = sent[c]
        held[c].append(swap(send, "fsdp", CHAINS[c][1][stage]))
        before = send if stage else before

    band = jnp.repeat(band, 4)[None]
    updated, coeffs, chosen = coefficients(held, momentum, band, low)
    fresh = new_momentum(updated, coeffs, low, momentum.shape)
    a, b, c, d = [chosen] + [swap(chosen, "rep", m) for m in (1, 8, 9)]
    summed = (a + b) + (c + d)
    parts = [summed] + [swap(summed, "rep", m) for m in (2, 4, 6)]
    scale = BLOCK / math.sqrt(BAND * lax.axis_size("rep"))
    update = make_update(parts, band, low, momentum.shape[2], scale)
    return (fresh, update)


def solution(mesh):
    in_specs = (P(("rep", "fsdp"), None), P(("rep", "fsdp"), None), P("rep", "fsdp", None), P())
    out_specs = (P("rep", "fsdp", None), P("fsdp", None))
    return jax.shard_map(
        per_device, mesh=mesh, in_specs=in_specs, out_specs=out_specs, check_vma=False
    )
```

```python
import functools
import math

import jax
import jax.numpy as jnp
import numpy as np
from jax import lax
from jax.experimental import pallas as pl
from jax.experimental.pallas import tpu as pltpu
from jax.sharding import PartitionSpec as P

BLOCK = 64
BAND = 32
LOW = 16
DECAY = 0.9
ROWS = 256
CHAINS = (
    (256, (12, 4, 1, 3)),
    (256, (4, 12, 3, 1)),
    (128, (4, 12, 1, 3)),
    (192, (3, 12, 4, 1)),
    (192, (1, 4, 3, 12)),
)
SCHEDULE = (
    (1, 0), (3, 0), (4, 0), (0, 0), (1, 1), (0, 1), (3, 1), (2, 0), (2, 1), (4, 1),
    (1, 2), (0, 2), (3, 2), (4, 2), (1, 3), (2, 2), (3, 3), (0, 3), (2, 3), (4, 3),
)
VMEM = 16 * 1024 * 1024
TERMS_VMEM = 50 * 1024 * 1024
IN_VMEM = pl.BlockSpec(memory_space=pltpu.VMEM)


def low_table():
    freq = np.arange(LOW, dtype=np.float64)[:, None]
    place = np.arange(BLOCK, dtype=np.float64)[None, :]
    factor = np.where(freq == 0, math.sqrt(1.0 / BLOCK), math.sqrt(2.0 / BLOCK))
    table = factor * np.cos(math.pi * (2.0 * place + 1.0) * freq / (2.0 * BLOCK))
    whole = np.kron(np.eye(ROWS // BLOCK), table).astype(np.float32)
    first = whole.astype(jnp.bfloat16)
    second = (whole - first.astype(np.float32)).astype(jnp.bfloat16)
    return np.concatenate([first, second], axis=0)


def swap(value, axis, mask):
    n = lax.axis_size(axis)
    return lax.ppermute(value, axis, [(i, i ^ mask) for i in range(n)])


def digits(offset, masks):
    for index in range(16):
        bits = [(index >> (3 - i)) & 1 for i in range(4)]
        if functools.reduce(lambda a, b: a ^ b, [m * b for m, b in zip(masks, bits)]) == offset:
            return index
    raise ValueError(offset)


def terms_kernel(kept, act_ref, cot_ref, *refs):
    outs = refs[: len(CHAINS)]
    gt_ref, buf_ref, cot_buf, sem_ref = refs[len(CHAINS) :]
    me = lax.axis_index("fsdp")
    a, b = me >> 2, me & 3
    width = buf_ref.shape[2]
    order = (0, 3, 1, 2) if kept else (2, 1, 3, 0)

    def load(ka):
        start = pl.multiple_of((a ^ ka) * width, width)
        return pltpu.make_async_copy(act_ref.at[:, pl.ds(start, width)], buf_ref.at[ka], sem_ref.at[ka])

    cot_copy = pltpu.make_async_copy(cot_ref, cot_buf, sem_ref.at[4])
    cot_copy.start()
    load(order[0]).start()
    cot_copy.wait()
    for ka in order[1:]:
        load(ka).start()
    gt_ref[...] = cot_buf[...].T
    for ka in order:
        load(ka).wait()
        for kb in range(4):
            offset = pl.multiple_of((b ^ kb) * ROWS, ROWS)
            runs, row = [], 0
            for c, (ncol, masks) in enumerate(CHAINS):
                index = digits(4 * ka + kb, masks)
                if (index < 8) == kept:
                    if runs and runs[-1][1] == row:
                        runs[-1][1] += ncol
                    else:
                        runs.append([row, row + ncol, []])
                    runs[-1][2].append((c, index % 8, ncol))
                row += ncol
            for first, last, members in runs:
                product = jnp.dot(
                    gt_ref[first:last, :], buf_ref[ka, :, pl.ds(offset, ROWS)], preferred_element_type=jnp.float32
                ).astype(jnp.bfloat16)
                at = 0
                for c, index, ncol in members:
                    outs[c][index] = product[at : at + ncol]
                    at += ncol


def terms(activations, cotangent, kept):
    tokens, width = activations.shape
    shapes = [jax.ShapeDtypeStruct((8, n, ROWS), jnp.bfloat16) for n, _ in CHAINS]
    return pl.pallas_call(
        functools.partial(terms_kernel, kept),
        in_specs=[
            pl.BlockSpec(memory_space=pltpu.HBM),
            pl.BlockSpec(memory_space=pltpu.HBM),
        ],
        out_specs=[IN_VMEM] * len(shapes),
        out_shape=shapes,
        scratch_shapes=[
            pltpu.VMEM((cotangent.shape[1], tokens), jnp.bfloat16),
            pltpu.VMEM((4, tokens, width // 4), jnp.bfloat16),
            pltpu.VMEM(cotangent.shape, jnp.bfloat16),
            pltpu.SemaphoreType.DMA((5,)),
        ],
        compiler_params=pltpu.CompilerParams(vmem_limit_bytes=(46 if kept else 50) * 2**20),
        cost_estimate=pl.CostEstimate(
            flops=tokens * width * cotangent.shape[1], bytes_accessed=tokens * width * 2, transcendentals=0
        ),
        name="terms_kept" if kept else "terms_sent",
    )(activations, cotangent)


def f32(x):
    return x.astype(jnp.float32)


def dot(a, b, dims=((1,), (0,))):
    return lax.dot_general(a, b, (dims, ((), ())), preferred_element_type=jnp.float32)


def split(x):
    first = x.astype(jnp.bfloat16)
    return first, (x - f32(first)).astype(jnp.bfloat16)


def forward(matrix, low):
    first, second = split(matrix)
    both = dot(low, first)
    left = both[:64] + both[64:] + dot(low[:64], second)
    stacked = jnp.concatenate([left[:, c : c + ROWS] for c in range(0, left.shape[1], ROWS)], axis=0)
    first, second = split(stacked)
    both = dot(first, low, ((1,), (1,)))
    return both[:, :64] + both[:, 64:] + dot(second, low[:64], ((1,), (1,)))


def backward(coeff, low):
    first, second = split(coeff)
    right = dot(first, low[:64]) + dot(first, low[64:]) + dot(second, low[:64])
    beside = jnp.concatenate([right[r : r + 64] for r in range(0, right.shape[0], 64)], axis=1)
    first, second = split(beside)
    three = jnp.concatenate([low, low[:64]], axis=0)
    return dot(three, jnp.concatenate([first, first, second], axis=0), ((0,), (0,)))


def add_kernel(size, *refs):
    for i in range(size):
        parts = [f32(ref[size + i]) for ref in refs[:-1]]
        refs[-1][i] = functools.reduce(jnp.add, parts).astype(jnp.bfloat16)


def add(held, size, name):
    _, rows, cols = held[0].shape
    return pl.pallas_call(
        functools.partial(add_kernel, size),
        in_specs=[IN_VMEM] * len(held),
        out_specs=IN_VMEM,
        out_shape=jax.ShapeDtypeStruct((size, rows, cols), jnp.bfloat16),
        compiler_params=pltpu.CompilerParams(vmem_limit_bytes=VMEM),
        cost_estimate=pl.CostEstimate(flops=size, bytes_accessed=size, transcendentals=0),
        name=name,
    )(*held)


def band_tables(band_ref, rows):
    width = 4 * BAND
    place = lax.broadcasted_iota(jnp.int32, (1, width), 1) // 4
    band = functools.reduce(jnp.add, [jnp.where(place == k, band_ref[k], 0) for k in range(BAND)])
    column = lax.broadcasted_iota(jnp.int32, (64, width), 1) % 4 * LOW + band % BLOCK
    pick = (lax.broadcasted_iota(jnp.int32, (64, width), 0) == column).astype(jnp.bfloat16)
    keep = (lax.broadcasted_iota(jnp.int32, (rows, width), 0) % LOW == band // BLOCK).astype(jnp.float32)
    own = lax.broadcasted_iota(jnp.int32, (rows // LOW, rows), 1) // LOW
    gather = (own == lax.broadcasted_iota(jnp.int32, (rows // LOW, rows), 0)).astype(jnp.bfloat16)
    return pick, keep, gather


def both_of(x, table, dims=((1,), (0,))):
    first, second = split(x)
    return dot(first, table, dims) + dot(second, table, dims)


def coeff_kernel(counts, *refs):
    n = sum(counts)
    mom_ref, band_ref, low_ref, updated_ref, coeff_ref, chosen_ref = refs[n:]
    rows, at = [], 0
    for count in counts:
        parts = [f32(ref[0]) for ref in refs[at : at + count]]
        rows.append(functools.reduce(jnp.add, parts))
        at += count
    gradient = jnp.concatenate(rows, axis=0)
    turned = [gradient[c : c + ROWS].T for c in range(0, gradient.shape[0], ROWS)]
    updated = DECAY * mom_ref[0] + jnp.concatenate(turned, axis=1)
    updated_ref[...] = updated
    coeff = forward(updated, low_ref[...])
    pick, keep, gather = band_tables(band_ref, coeff.shape[0])
    picked = both_of(coeff, pick) * keep
    first, second = split(picked)
    chosen_ref[...] = dot(gather, first) + dot(gather, second)
    coeff_ref[...] = both_of(picked, pick, ((1,), (1,)))


def coefficients(held, momentum, band, low):
    _, rows, ncol = momentum.shape
    arrays = [a for chain in held for a in chain]
    return pl.pallas_call(
        functools.partial(coeff_kernel, [len(chain) for chain in held]),
        in_specs=[IN_VMEM] * (len(arrays) + 1) + [pl.BlockSpec(memory_space=pltpu.SMEM), IN_VMEM],
        out_specs=[IN_VMEM] * 3,
        out_shape=[
            jax.ShapeDtypeStruct((rows, ncol), jnp.float32),
            jax.ShapeDtypeStruct((ncol // 4, 64), jnp.float32),
            jax.ShapeDtypeStruct((ncol // 64, 4 * BAND), jnp.float32),
        ],
        compiler_params=pltpu.CompilerParams(vmem_limit_bytes=VMEM),
        cost_estimate=pl.CostEstimate(flops=ncol * 1000000, bytes_accessed=ncol * 256 * 8, transcendentals=0),
        name="coefficients",
    )(*arrays, momentum, band, low)


def fresh_kernel(updated_ref, coeff_ref, low_ref, out_ref):
    out_ref[0] = updated_ref[...] - backward(coeff_ref[...], low_ref[...])


def new_momentum(updated, coeffs, low, shape):
    return pl.pallas_call(
        fresh_kernel,
        in_specs=[IN_VMEM] * 3,
        out_shape=jax.ShapeDtypeStruct(shape, jnp.float32),
        compiler_params=pltpu.CompilerParams(vmem_limit_bytes=VMEM),
        cost_estimate=pl.CostEstimate(flops=2000000000, bytes_accessed=2000000, transcendentals=0),
        name="new_momentum",
    )(updated, coeffs, low)


def update_kernel(scale, a_ref, b_ref, c_ref, d_ref, band_ref, low_ref, out_ref):
    total = (a_ref[...] + b_ref[...]) + (c_ref[...] + d_ref[...])
    pick, keep, gather = band_tables(band_ref, LOW * total.shape[0])
    first, second = split(total)
    spread = (dot(gather, first, ((0,), (0,))) + dot(gather, second, ((0,), (0,)))) * keep
    coeff = both_of(spread, pick, ((1,), (1,)))
    out_ref[...] = (backward(coeff, low_ref[...]) * scale).astype(jnp.bfloat16)


def make_update(parts, band, low, ncols, scale):
    return pl.pallas_call(
        functools.partial(update_kernel, scale),
        in_specs=[IN_VMEM] * 4 + [pl.BlockSpec(memory_space=pltpu.SMEM), IN_VMEM],
        out_shape=jax.ShapeDtypeStruct((ROWS, ncols), jnp.bfloat16),
        compiler_params=pltpu.CompilerParams(vmem_limit_bytes=VMEM),
        name="update",
    )(*parts, band, low)


def per_device(activations, cotangent, momentum, band):
    low = jnp.asarray(low_table())
    sent = terms(activations, cotangent, False)
    cotangent, _ = lax.optimization_barrier((cotangent, sent[0]))
    kept = terms(activations, cotangent, True)
    held = [[k] for k in kept]
    before = sent[0]
    for c, stage in SCHEDULE:
        if stage:
            held[c][-1], before = lax.optimization_barrier((held[c][-1], before))
            send = add(held[c], 8 >> stage, "add%d_%d" % (c, stage))
        else:
            send = sent[c]
        held[c].append(swap(send, "fsdp", CHAINS[c][1][stage]))
        before = send if stage else before

    updated, coeffs, chosen = coefficients(held, momentum, band, low)
    fresh = new_momentum(updated, coeffs, low, momentum.shape)
    a, b, c, d = [chosen] + [swap(chosen, "rep", m) for m in (1, 8, 9)]
    summed = (a + b) + (c + d)
    parts = [summed] + [swap(summed, "rep", m) for m in (2, 4, 6)]
    scale = BLOCK / math.sqrt(BAND * lax.axis_size("rep"))
    update = make_update(parts, band, low, momentum.shape[2], scale)
    return (fresh, update)


def solution(mesh):
    in_specs = (P(("rep", "fsdp"), None), P(("rep", "fsdp"), None), P("rep", "fsdp", None), P())
    out_specs = (P("rep", "fsdp", None), P("fsdp", None))
    return jax.shard_map(
        per_device, mesh=mesh, in_specs=in_specs, out_specs=out_specs, check_vma=False
    )
```

```python
import functools
import math

import jax
import jax.numpy as jnp
import numpy as np
from jax import lax
from jax.experimental import pallas as pl
from jax.experimental.pallas import tpu as pltpu
from jax.sharding import PartitionSpec as P

BLOCK = 64
BAND = 32
LOW = 16
DECAY = 0.9
ROWS = 256
CHAINS = (
    (256, (12, 4, 1, 3)),
    (256, (4, 12, 3, 1)),
    (128, (4, 12, 1, 3)),
    (192, (3, 12, 4, 1)),
    (192, (1, 4, 3, 12)),
)
SCHEDULE = (
    (1, 0), (3, 0), (4, 0), (0, 0), (1, 1), (0, 1), (3, 1), (2, 0), (2, 1), (4, 1),
    (1, 2), (0, 2), (3, 2), (4, 2), (1, 3), (2, 2), (3, 3), (0, 3), (2, 3), (4, 3),
)
VMEM = 16 * 1024 * 1024
TERMS_VMEM = 50 * 1024 * 1024
IN_VMEM = pl.BlockSpec(memory_space=pltpu.VMEM)


def low_table():
    freq = np.arange(LOW, dtype=np.float64)[:, None]
    place = np.arange(BLOCK, dtype=np.float64)[None, :]
    factor = np.where(freq == 0, math.sqrt(1.0 / BLOCK), math.sqrt(2.0 / BLOCK))
    table = factor * np.cos(math.pi * (2.0 * place + 1.0) * freq / (2.0 * BLOCK))
    whole = np.kron(np.eye(ROWS // BLOCK), table).astype(np.float32)
    first = whole.astype(jnp.bfloat16)
    second = (whole - first.astype(np.float32)).astype(jnp.bfloat16)
    return np.concatenate([first, second], axis=0)


def swap(value, axis, mask):
    n = lax.axis_size(axis)
    return lax.ppermute(value, axis, [(i, i ^ mask) for i in range(n)])


def digits(offset, masks):
    for index in range(16):
        bits = [(index >> (3 - i)) & 1 for i in range(4)]
        if functools.reduce(lambda a, b: a ^ b, [m * b for m, b in zip(masks, bits)]) == offset:
            return index
    raise ValueError(offset)


def terms_kernel(kept, act_ref, cot_ref, *refs):
    outs = refs[: len(CHAINS)]
    gt_ref, buf_ref, cot_buf, sem_ref = refs[len(CHAINS) :]
    me = lax.axis_index("fsdp")
    a, b = me >> 2, me & 3
    width = buf_ref.shape[2]
    order = (0, 3, 1, 2) if kept else (2, 1, 3, 0)

    def load(ka):
        start = pl.multiple_of((a ^ ka) * width, width)
        return pltpu.make_async_copy(act_ref.at[:, pl.ds(start, width)], buf_ref.at[ka], sem_ref.at[ka])

    cot_copy = pltpu.make_async_copy(cot_ref, cot_buf, sem_ref.at[4])
    cot_copy.start()
    load(order[0]).start()
    cot_copy.wait()
    for ka in order[1:]:
        load(ka).start()
    gt_ref[...] = cot_buf[...].T
    for ka in order:
        load(ka).wait()
        for kb in range(4):
            offset = pl.multiple_of((b ^ kb) * ROWS, ROWS)
            runs, row = [], 0
            for c, (ncol, masks) in enumerate(CHAINS):
                index = digits(4 * ka + kb, masks)
                if (index < 8) == kept:
                    if runs and runs[-1][1] == row:
                        runs[-1][1] += ncol
                    else:
                        runs.append([row, row + ncol, []])
                    runs[-1][2].append((c, index % 8, ncol))
                row += ncol
            for first, last, members in runs:
                product = jnp.dot(
                    gt_ref[first:last, :], buf_ref[ka, :, pl.ds(offset, ROWS)], preferred_element_type=jnp.float32
                ).astype(jnp.bfloat16)
                at = 0
                for c, index, ncol in members:
                    outs[c][index] = product[at : at + ncol]
                    at += ncol


def terms(activations, cotangent, kept):
    tokens, width = activations.shape
    shapes = [jax.ShapeDtypeStruct((8, n, ROWS), jnp.bfloat16) for n, _ in CHAINS]
    return pl.pallas_call(
        functools.partial(terms_kernel, kept),
        in_specs=[
            pl.BlockSpec(memory_space=pltpu.HBM),
            pl.BlockSpec(memory_space=pltpu.HBM),
        ],
        out_specs=[IN_VMEM] * len(shapes),
        out_shape=shapes,
        scratch_shapes=[
            pltpu.VMEM((cotangent.shape[1], tokens), jnp.bfloat16),
            pltpu.VMEM((4, tokens, width // 4), jnp.bfloat16),
            pltpu.VMEM(cotangent.shape, jnp.bfloat16),
            pltpu.SemaphoreType.DMA((5,)),
        ],
        compiler_params=pltpu.CompilerParams(vmem_limit_bytes=(46 if kept else 50) * 2**20),
        cost_estimate=pl.CostEstimate(
            flops=tokens * width * cotangent.shape[1], bytes_accessed=tokens * width * 2, transcendentals=0
        ),
        name="terms_kept" if kept else "terms_sent",
    )(activations, cotangent)


def f32(x):
    return x.astype(jnp.float32)


def dot(a, b, dims=((1,), (0,))):
    return lax.dot_general(a, b, (dims, ((), ())), preferred_element_type=jnp.float32)


def split(x):
    first = x.astype(jnp.bfloat16)
    return first, (x - f32(first)).astype(jnp.bfloat16)


def forward(matrix, low):
    first, second = split(matrix)
    both = dot(low, first)
    left = both[:64] + both[64:] + dot(low[:64], second)
    stacked = jnp.concatenate([left[:, c : c + ROWS] for c in range(0, left.shape[1], ROWS)], axis=0)
    first, second = split(stacked)
    both = dot(first, low, ((1,), (1,)))
    return both[:, :64] + both[:, 64:] + dot(second, low[:64], ((1,), (1,)))


def backward(coeff, low):
    first, second = split(coeff)
    right = dot(first, low[:64]) + dot(first, low[64:]) + dot(second, low[:64])
    beside = jnp.concatenate([right[r : r + 64] for r in range(0, right.shape[0], 64)], axis=1)
    first, second = split(beside)
    three = jnp.concatenate([low, low[:64]], axis=0)
    return dot(three, jnp.concatenate([first, first, second], axis=0), ((0,), (0,)))


def add_kernel(size, *refs):
    for i in range(size):
        parts = [f32(ref[size + i]) for ref in refs[:-1]]
        refs[-1][i] = functools.reduce(jnp.add, parts).astype(jnp.bfloat16)


def add(held, size, name):
    _, rows, cols = held[0].shape
    return pl.pallas_call(
        functools.partial(add_kernel, size),
        in_specs=[IN_VMEM] * len(held),
        out_specs=IN_VMEM,
        out_shape=jax.ShapeDtypeStruct((size, rows, cols), jnp.bfloat16),
        compiler_params=pltpu.CompilerParams(vmem_limit_bytes=VMEM),
        cost_estimate=pl.CostEstimate(flops=size, bytes_accessed=size, transcendentals=0),
        name=name,
    )(*held)


def band_tables(band_ref, rows):
    width = 4 * BAND
    place = lax.broadcasted_iota(jnp.int32, (1, width), 1) // 4
    band = functools.reduce(jnp.add, [jnp.where(place == k, band_ref[k], 0) for k in range(BAND)])
    column = lax.broadcasted_iota(jnp.int32, (64, width), 1) % 4 * LOW + band % BLOCK
    pick = (lax.broadcasted_iota(jnp.int32, (64, width), 0) == column).astype(jnp.bfloat16)
    keep = (lax.broadcasted_iota(jnp.int32, (rows, width), 0) % LOW == band // BLOCK).astype(jnp.float32)
    own = lax.broadcasted_iota(jnp.int32, (rows // LOW, rows), 1) // LOW
    gather = (own == lax.broadcasted_iota(jnp.int32, (rows // LOW, rows), 0)).astype(jnp.bfloat16)
    own = lax.broadcasted_iota(jnp.int32, (rows, rows // LOW), 0) // LOW
    spread = (own == lax.broadcasted_iota(jnp.int32, (rows, rows // LOW), 1)).astype(jnp.bfloat16)
    return pick, keep, gather, spread


def both_of(x, table, dims=((1,), (0,))):
    first, second = split(x)
    return dot(first, table, dims) + dot(second, table, dims)


def coeff_kernel(counts, *refs):
    n = sum(counts)
    mom_ref, band_ref, low_ref, updated_ref, coeff_ref, chosen_ref, pick_ref, keep_ref, spread_ref = refs[n:]
    rows, at = [], 0
    for count in counts:
        parts = [f32(ref[0]) for ref in refs[at : at + count]]
        rows.append(functools.reduce(jnp.add, parts))
        at += count
    gradient = jnp.concatenate(rows, axis=0)
    turned = [gradient[c : c + ROWS].T for c in range(0, gradient.shape[0], ROWS)]
    updated = DECAY * mom_ref[0] + jnp.concatenate(turned, axis=1)
    updated_ref[...] = updated
    coeff = forward(updated, low_ref[...])
    pick, keep, gather, spread = band_tables(band_ref, coeff.shape[0])
    pick_ref[...], keep_ref[...], spread_ref[...] = pick, keep, spread
    picked = both_of(coeff, pick) * keep
    first, second = split(picked)
    chosen_ref[...] = dot(gather, first) + dot(gather, second)
    coeff_ref[...] = both_of(picked, pick, ((1,), (1,)))


def coefficients(held, momentum, band, low):
    _, rows, ncol = momentum.shape
    arrays = [a for chain in held for a in chain]
    return pl.pallas_call(
        functools.partial(coeff_kernel, [len(chain) for chain in held]),
        in_specs=[IN_VMEM] * (len(arrays) + 1) + [pl.BlockSpec(memory_space=pltpu.SMEM), IN_VMEM],
        out_specs=[IN_VMEM] * 6,
        out_shape=[
            jax.ShapeDtypeStruct((rows, ncol), jnp.float32),
            jax.ShapeDtypeStruct((ncol // 4, 64), jnp.float32),
            jax.ShapeDtypeStruct((ncol // 64, 4 * BAND), jnp.float32),
            jax.ShapeDtypeStruct((64, 4 * BAND), jnp.bfloat16),
            jax.ShapeDtypeStruct((ncol // 4, 4 * BAND), jnp.float32),
            jax.ShapeDtypeStruct((ncol // 4, ncol // 64), jnp.bfloat16),
        ],
        compiler_params=pltpu.CompilerParams(vmem_limit_bytes=VMEM),
        cost_estimate=pl.CostEstimate(flops=ncol * 1000000, bytes_accessed=ncol * 256 * 8, transcendentals=0),
        name="coefficients",
    )(*arrays, momentum, band, low)


def fresh_kernel(updated_ref, coeff_ref, low_ref, out_ref):
    out_ref[0] = updated_ref[...] - backward(coeff_ref[...], low_ref[...])


def new_momentum(updated, coeffs, low, shape):
    return pl.pallas_call(
        fresh_kernel,
        in_specs=[IN_VMEM] * 3,
        out_shape=jax.ShapeDtypeStruct(shape, jnp.float32),
        compiler_params=pltpu.CompilerParams(vmem_limit_bytes=VMEM),
        cost_estimate=pl.CostEstimate(flops=2000000000, bytes_accessed=2000000, transcendentals=0),
        name="new_momentum",
    )(updated, coeffs, low)


def update_kernel(scale, a_ref, b_ref, c_ref, d_ref, pick_ref, keep_ref, spread_ref, low_ref, out_ref):
    total = (a_ref[...] + b_ref[...]) + (c_ref[...] + d_ref[...])
    first, second = split(total)
    repeated = (dot(spread_ref[...], first) + dot(spread_ref[...], second)) * keep_ref[...]
    coeff = both_of(repeated, pick_ref[...], ((1,), (1,)))
    out_ref[...] = (backward(coeff, low_ref[...]) * scale).astype(jnp.bfloat16)


def make_update(parts, tables, low, ncols, scale):
    return pl.pallas_call(
        functools.partial(update_kernel, scale),
        in_specs=[IN_VMEM] * 8,
        out_shape=jax.ShapeDtypeStruct((ROWS, ncols), jnp.bfloat16),
        compiler_params=pltpu.CompilerParams(vmem_limit_bytes=VMEM),
        name="update",
    )(*parts, *tables, low)


def per_device(activations, cotangent, momentum, band):
    low = jnp.asarray(low_table())
    sent = terms(activations, cotangent, False)
    cotangent, _ = lax.optimization_barrier((cotangent, sent[0]))
    kept = terms(activations, cotangent, True)
    held = [[k] for k in kept]
    before = sent[0]
    for c, stage in SCHEDULE:
        if stage:
            held[c][-1], before = lax.optimization_barrier((held[c][-1], before))
            send = add(held[c], 8 >> stage, "add%d_%d" % (c, stage))
        else:
            send = sent[c]
        held[c].append(swap(send, "fsdp", CHAINS[c][1][stage]))
        before = send if stage else before

    updated, coeffs, chosen, *tables = coefficients(held, momentum, band, low)
    fresh = new_momentum(updated, coeffs, low, momentum.shape)
    a, b, c, d = [chosen] + [swap(chosen, "rep", m) for m in (1, 8, 9)]
    summed = (a + b) + (c + d)
    parts = [summed] + [swap(summed, "rep", m) for m in (2, 4, 6)]
    scale = BLOCK / math.sqrt(BAND * lax.axis_size("rep"))
    update = make_update(parts, tables, low, momentum.shape[2], scale)
    return (fresh, update)


def solution(mesh):
    in_specs = (P(("rep", "fsdp"), None), P(("rep", "fsdp"), None), P("rep", "fsdp", None), P())
    out_specs = (P("rep", "fsdp", None), P("fsdp", None))
    return jax.shard_map(
        per_device, mesh=mesh, in_specs=in_specs, out_specs=out_specs, check_vma=False
    )
```
